256 devices in a mesh: member: 4 (over y), band: 64 (over x, z, core).
Axes of the slice: x: 4, y: 4, z: 8, core: 2. Of those that a mesh axis runs over, the one named last changes fastest.
Arguments:
- predicted_states: bfloat16 [16, 100, 128, 1440], P('member', None, 'band'), may hold values from -6 to 6
- observed_truth: bfloat16 [100, 128, 1440], P(None, 'band', 'member'), may hold values from -6 to 6
- height_penalty_factor: float32 [100], replicated, may hold values from 0.5 to 5
Outputs:
- member_grad: bfloat16 [16, 100, 128, 1440], P('member', None, 'band')
- variable_loss: float32 [100], replicated
The draws below stay inside these ranges and needn't reach their ends.
All inputs are finite; a program needn't handle non-finite values.
Results may differ from the reference program's by a relative error of at most 0.0055.
Values may be sent and summed in bfloat16 or wider, within the bound.
A program may use at most 64 MiB of HBM per device.

```python
import math
import jax
import jax.numpy as jnp
from jax import lax

ENSEMBLE_SIZE = 16
QUANTITY_HEIGHTS = 100
MERIDIAN_CELLS = 1440
PARALLEL_BANDS = 128


def level_of(key, shape, cuts, least, top_value):
    factor_of = 1.0
    for axis_at, shards_of in cuts:
        heights = jax.random.uniform(jax.random.fold_in(jax.random.fold_in(key, 6), axis_at), (shards_of,), jnp.float32, least / len(cuts), top_value / len(cuts))
        factor_of = factor_of * jnp.repeat(jnp.exp(heights), shape[axis_at] // shards_of).reshape((-1,) + (1,) * (len(shape) - 1 - axis_at))
    return factor_of


def gaussian(rng, extent, spread, most, pieces=(), kind=jnp.bfloat16):
    drawn = jax.random.normal(rng, extent, jnp.float32) * spread
    if len(pieces) > 0:
        drawn = level_of(rng, extent, pieces, -0.22, 0.18) * drawn
    return jnp.clip(drawn, min=-most, max=most).astype(kind)


def setup_inputs(seed: int = 0) -> dict:
    arg_keys = jax.random.split(jax.random.key(seed), 4)
    predicted_states = gaussian(arg_keys[0], (ENSEMBLE_SIZE, QUANTITY_HEIGHTS, PARALLEL_BANDS, MERIDIAN_CELLS), 1.0, 6.0, ((0, 4), (2, 64)))
    observed_truth = gaussian(arg_keys[1], (QUANTITY_HEIGHTS, PARALLEL_BANDS, MERIDIAN_CELLS), 1.0, 6.0, ((1, 64), (2, 4)))
    height_penalty_factor = jnp.clip(jnp.exp(jax.random.uniform(arg_keys[2], (QUANTITY_HEIGHTS,), jnp.float32, math.log(0.5), math.log(5.0))), 0.5, 5.0)
    return {"predicted_states": predicted_states, "observed_truth": observed_truth, "height_penalty_factor": height_penalty_factor}


alpha_fair = 0.95


def row_areas(parallel_band_sum):
    positions = jnp.arange(parallel_band_sum, dtype=jnp.float32)
    latitude = 0.5 * math.pi - math.pi * (positions + 0.5) / parallel_band_sum
    cosines = jnp.cos(latitude)
    return cosines / jnp.mean(cosines)


def reference(predicted_states, observed_truth, height_penalty_factor):
    ensemble_collection = ENSEMBLE_SIZE
    fair = 1.0 - (1.0 - alpha_fair) / ensemble_collection
    areas = row_areas(PARALLEL_BANDS)

    def lone_quantity(inputs):
        field, observed, weight = inputs
        ensemble = field.astype(jnp.float32)
        truth_field = observed.astype(jnp.float32)
        sign_sum = jnp.zeros(ensemble.shape, jnp.float32)
        abs_sum = jnp.zeros(ensemble.shape, jnp.float32)
        for other in range(ensemble_collection):
            differ = ensemble - ensemble[other]
            sign_sum = sign_sum + jnp.sign(differ)
            abs_sum = abs_sum + jnp.abs(differ)
        scale = weight * areas[None, :, None]
        gradient = scale * (jnp.sign(ensemble - truth_field[None]) / ensemble_collection - fair * sign_sum / (ensemble_collection * (ensemble_collection - 1)))
        terms = areas[None, :, None] * (jnp.abs(ensemble - truth_field[None]) / ensemble_collection - fair * abs_sum / (2 * ensemble_collection * (ensemble_collection - 1)))
        return gradient.astype(jnp.bfloat16), jnp.sum(terms)

    derivative_maps, accumulated_sums = lax.map(lone_quantity, (jnp.moveaxis(predicted_states, 1, 0), observed_truth, height_penalty_factor))
    return jnp.moveaxis(derivative_maps, 0, 1), height_penalty_factor * accumulated_sums / (PARALLEL_BANDS * MERIDIAN_CELLS)
```

```python
import functools
import math

import jax
import jax.numpy as jnp
import numpy as np
from jax import lax
from jax.experimental import pallas as pl
from jax.experimental.pallas import tpu as pltpu
from jax.sharding import PartitionSpec as P

MESH = pl.DeviceIdType.MESH
ALPHA_FAIR = 0.95
UP = 2.0**120
STEP = 2.0**-13
HALVES = ((0, 1024), (1024, 416))
Z, CORES = 8, 2


def mean_cosine(rows):
    positions = np.arange(rows, dtype=np.float64)
    return float(np.mean(np.cos(0.5 * math.pi - math.pi * (positions + 0.5) / rows)))


def rank_points(members, truth, truth32, weighted, member_value, put):
    count = len(members)
    fair = 1.0 - (1.0 - ALPHA_FAIR) / count
    low, high = jnp.bfloat16(-STEP), jnp.bfloat16(STEP)
    up = [m * jnp.bfloat16(UP) for m in members]
    truth_up = truth * jnp.bfloat16(UP)
    signs = [None] * count
    for j in range(count):
        for k in range(j + 1, count):
            s = jnp.minimum(jnp.maximum(up[j] - up[k], low), high)
            signs[j] = s if signs[j] is None else signs[j] + s
            signs[k] = -s if signs[k] is None else signs[k] - s
    total = None
    for j in range(count):
        beside = jnp.minimum(jnp.maximum(up[j] - truth_up, low), high).astype(jnp.float32)
        grad = beside * (1.0 / STEP / count) - signs[j].astype(jnp.float32) * (
            fair / STEP / (count * (count - 1))
        )
        term = (member_value(j).astype(jnp.float32) - truth32) * grad
        total = term if total is None else total + term
        put(j, (weighted * grad).astype(jnp.bfloat16))
    return total


def kernel(sizes, x_ref, t_ref, w_ref, y_ref, loss_ref, xs, ts, tf, ys, area, part, near, far, ring, *sems):
    members, levels, rows, cells, groups, bands, chunks = sizes
    own, deep = levels // groups, levels // groups // chunks
    (x_send, x_recv, x_sem, t_send, t_recv, t_sem, y_send, y_recv, y_sem, l_send, l_recv) = sems
    me, band = lax.axis_index("member"), lax.axis_index("band")
    core, z, x = lax.rem(band, CORES), lax.rem(band // CORES, Z), band // (CORES * Z)
    xs_count = bands // (CORES * Z)
    nears, fars = xs_count * CORES, Z
    near_me = x * CORES + core

    def member_at(d):
        return {"member": lax.rem(me + d, groups)}

    def near_at(d):
        i = lax.rem(near_me + d, nears)
        return i, {"band": ((i // CORES) * Z + z) * CORES + lax.rem(i, CORES)}

    def far_at(d):
        i = lax.rem(z + d, fars)
        return i, {"band": (x * Z + i) * CORES + core}

    peers = [member_at(d) for d in range(1, groups)]
    peers += [near_at(d)[1] for d in range(1, nears)]
    peers += [far_at(d)[1] for d in range(1, fars)]
    barrier = pltpu.get_barrier_semaphore()
    for peer in peers:
        pl.semaphore_signal(barrier, inc=1, device_id=peer, device_id_type=MESH)
    pl.semaphore_wait(barrier, len(peers))

    def send_t(d):
        return pltpu.make_async_remote_copy(
            t_ref.at[pl.ds(own * lax.rem(me + d, groups), own)], ts.at[me],
            t_send.at[d - 1], t_recv.at[d - 1], device_id=member_at(d), device_id_type=MESH,
        )

    def send_x(d, c):
        return pltpu.make_async_remote_copy(
            x_ref.at[:, pl.ds(own * lax.rem(me + d, groups) + deep * c, deep)],
            xs.at[groups - d, :, pl.ds(deep * c, deep)],
            x_send.at[d - 1, c], x_recv.at[d - 1, c], device_id=member_at(d), device_id_type=MESH,
        )

    def send_y(d, c):
        return pltpu.make_async_remote_copy(
            ys.at[d, :, pl.ds(deep * c, deep)],
            y_ref.at[:, pl.ds(own * me + deep * c, deep)],
            y_send.at[d - 1, c], y_recv.at[d - 1, c], device_id=member_at(d), device_id_type=MESH,
        )

    order = (1, 3, 2)
    keep_t = pltpu.make_async_copy(t_ref.at[pl.ds(own * me, own)], ts.at[me], t_sem)
    keep_x = pltpu.make_async_copy(x_ref.at[:, pl.ds(own * me, own)], xs.at[0], x_sem)
    for d in order:
        send_t(d).start()
    for c in range(chunks):
        for d in order:
            send_x(d, c).start()
        if c == 0:
            keep_t.start()
            keep_x.start()

    lat = 0.5 * math.pi - (math.pi / (bands * rows)) * (
        (lax.broadcasted_iota(jnp.int32, (rows, cells), 0) + band * rows).astype(jnp.float32) + 0.5
    )
    area[...] = jnp.cos(lat) * (1.0 / mean_cosine(bands * rows))
    part[...] = jnp.zeros_like(part)
    lanes = lax.broadcasted_iota(jnp.int32, (8, 128), 1)

    keep_t.wait()
    keep_x.wait()
    for d in order:
        send_t(d).wait_recv()

    def widen(v, carry):
        tf[v] = jnp.concatenate([ts[p, v].astype(jnp.float32) for p in range(groups)], axis=-1)
        return carry

    lax.fori_loop(0, own, widen, 0)

    def level(v, carry):
        weight = w_ref[own * me + v]
        loss = None
        for start, size in HALVES:
            cut = pl.ds(start, size)
            truth32 = tf[v, :, cut]
            area_here = area[:, cut]

            def member_value(j):
                return xs[j // members, j % members, v, :, cut]

            def put(j, value):
                ys[j // members, j % members, v, :, cut] = value

            total = rank_points(
                [member_value(j) for j in range(groups * members)],
                truth32.astype(jnp.bfloat16), truth32, weight * area_here, member_value, put,
            )
            total = jnp.sum(total * area_here)
            loss = total if loss is None else loss + total
        loss = loss * weight * (1.0 / (bands * rows * cells))
        part[...] += jnp.where(lanes == own * me + v, loss, 0.0)
        return carry

    def chunk(c, carry):
        for d in order:
            send_x(d, c).wait_recv()
        lax.fori_loop(c * deep, (c + 1) * deep, level, 0)
        for d in order:
            send_y(d, c).start()
        return carry

    lax.fori_loop(0, chunks, chunk, 0)
    keep_y = pltpu.make_async_copy(ys.at[0], y_ref.at[:, pl.ds(own * me, own)], y_sem)
    keep_y.start()

    def exchange(slots, count, mine, at, base):
        slots[mine] = part[...]

        def copy(d):
            i, peer = at(d)
            return pltpu.make_async_remote_copy(
                part, slots.at[mine], l_send.at[base + d], l_recv.at[base + d], device_id=peer, device_id_type=MESH,
            )

        for d in range(1, count):
            copy(d).start()
        for d in range(1, count):
            copy(d).wait()
        total = slots[0]
        for i in range(1, count):
            total = total + slots[i]
        part[...] = total

    exchange(near, nears, near_me, near_at, 0)
    exchange(far, fars, z, far_at, nears)
    exchange(ring, groups, me, lambda d: (d, member_at(d)), nears + fars)
    loss_ref[...] = part[0, :levels]

    for d in order:
        send_t(d).wait_send()

    def drain(c, carry):
        for d in order:
            send_x(d, c).wait_send()
            send_y(d, c).wait()
        return carry

    lax.fori_loop(0, chunks, drain, 0)
    keep_y.wait()


def solution(mesh):
    groups, bands = mesh.shape["member"], mesh.shape["band"]
    chunks = 5

    def on_device(predicted_states, observed_truth, height_penalty_factor):
        members, levels, rows, cells = predicted_states.shape
        own = levels // groups
        sizes = (members, levels, rows, cells, groups, bands, chunks)
        nears, fars = bands // Z, Z
        dma = pltpu.SemaphoreType.DMA
        peers = nears + fars + groups
        return pl.pallas_call(
            functools.partial(kernel, sizes),
            out_shape=(
                jax.ShapeDtypeStruct(predicted_states.shape, jnp.bfloat16),
                jax.ShapeDtypeStruct((levels,), jnp.float32),
            ),
            in_specs=[pl.BlockSpec(memory_space=pltpu.HBM)] * 2 + [pl.BlockSpec(memory_space=pltpu.SMEM)],
            out_specs=(pl.BlockSpec(memory_space=pl.ANY), pl.BlockSpec(memory_space=pltpu.VMEM)),
            scratch_shapes=[
                pltpu.VMEM((groups, members, own, rows, cells), jnp.bfloat16),
                pltpu.VMEM((groups, own, rows, cells // groups), jnp.bfloat16),
                pltpu.VMEM((own, rows, cells), jnp.float32),
                pltpu.VMEM((groups, members, own, rows, cells), jnp.bfloat16),
                pltpu.VMEM((rows, cells), jnp.float32),
                pltpu.VMEM((8, 128), jnp.float32),
                pltpu.VMEM((nears, 8, 128), jnp.float32),
                pltpu.VMEM((fars, 8, 128), jnp.float32),
                pltpu.VMEM((groups, 8, 128), jnp.float32),
                dma((groups - 1, chunks)), dma((groups - 1, chunks)), dma,
                dma((groups - 1,)), dma((groups - 1,)), dma,
                dma((groups - 1, chunks)), dma((groups - 1, chunks)), dma,
                dma((peers,)), dma((peers,)),
            ],
            compiler_params=pltpu.CompilerParams(
                collective_id=0, has_side_effects=True, vmem_limit_bytes=56 * 2**20
            ),
        )(predicted_states, observed_truth, height_penalty_factor)

    in_specs = (P("member", None, "band", None), P(None, "band", "member"), P())
    out_specs = (P("member", None, "band", None), P())
    return jax.shard_map(on_device, mesh=mesh, in_specs=in_specs, out_specs=out_specs, check_vma=False)
```

```python
import functools
import math

import jax
import jax.numpy as jnp
import numpy as np
from jax import lax
from jax.experimental import pallas as pl
from jax.experimental.pallas import tpu as pltpu
from jax.sharding import PartitionSpec as P

MESH = pl.DeviceIdType.MESH
ALPHA_FAIR = 0.95
UP = 2.0**120
STEP = 2.0**-13
HALVES = ((0, 1024), (1024, 416))
Z, CORES = 8, 2


def mean_cosine(rows):
    positions = np.arange(rows, dtype=np.float64)
    return float(np.mean(np.cos(0.5 * math.pi - math.pi * (positions + 0.5) / rows)))


def rank_points(members, truth, truth32, weighted, member_value, put):
    count = len(members)
    fair = 1.0 - (1.0 - ALPHA_FAIR) / count
    low, high = jnp.bfloat16(-STEP), jnp.bfloat16(STEP)
    up = [m * jnp.bfloat16(UP) for m in members]
    truth_up = truth * jnp.bfloat16(UP)
    signs = [None] * count
    for j in range(count):
        for k in range(j + 1, count):
            s = jnp.minimum(jnp.maximum(up[j] - up[k], low), high)
            signs[j] = s if signs[j] is None else signs[j] + s
            signs[k] = -s if signs[k] is None else signs[k] - s
    total = None
    for j in range(count):
        beside = jnp.minimum(jnp.maximum(up[j] - truth_up, low), high).astype(jnp.float32)
        grad = beside * (1.0 / STEP / count) - signs[j].astype(jnp.float32) * (
            fair / STEP / (count * (count - 1))
        )
        term = (member_value(j).astype(jnp.float32) - truth32) * grad
        total = term if total is None else total + term
        put(j, (weighted * grad).astype(jnp.bfloat16))
    return total


def kernel(sizes, x_ref, t_ref, w_ref, y_ref, loss_ref, xs, ts, tf, ys, area, part, ring, near, far, ready, opened, *sems):
    members, levels, rows, cells, groups, bands, chunks = sizes
    own, deep = levels // groups, levels // groups // chunks
    (x_send, x_recv, x_sem, t_send, t_recv, t_sem, y_send, y_recv, y_sem, l_send, l_recv) = sems
    me, band = lax.axis_index("member"), lax.axis_index("band")
    core, z, x = lax.rem(band, CORES), lax.rem(band // CORES, Z), band // (CORES * Z)
    wide, tall = bands // (CORES * Z), Z

    def member_at(d):
        return {"member": lax.rem(me + d, groups)}

    def across(d):
        return {"band": (lax.rem(x + d, wide) * Z + z) * CORES + core}

    def around(d):
        i = lax.rem(x * CORES + core + d, wide * CORES)
        return {"band": ((i // CORES) * Z + z) * CORES + lax.rem(i, CORES)}

    def along(d):
        return {"band": (x * Z + lax.rem(z + d, tall)) * CORES + core}

    partner = {"band": band + 1 - 2 * core}
    head = (me == 0) & (core == 0)
    heads = [across(d) for d in range(1, wide)] + [along(d) for d in range(1, tall)]

    barrier = pltpu.get_barrier_semaphore()

    def greet(sem, peer):
        pl.semaphore_signal(sem, inc=1, device_id=peer, device_id_type=MESH)

    for d in range(1, groups):

        @pl.when(jnp.logical_not((lax.rem(me + d, groups) == 0) & (core == 0)))
        def _():
            greet(barrier, member_at(d))

    @pl.when(jnp.logical_not((me == 0) & (core == 1)))
    def _():
        greet(barrier, partner)

    @pl.when(jnp.logical_not(head))
    def _():
        pl.semaphore_wait(barrier, groups)

        @pl.when(core == 0)
        def _():
            greet(ready, {"member": 0})

        @pl.when(me == 0)
        def _():
            greet(ready, partner)

    @pl.when(head)
    def _():
        pl.semaphore_wait(ready, groups)
        for peer in heads:
            greet(barrier, peer)

    def send_t(d):
        return pltpu.make_async_remote_copy(
            t_ref.at[pl.ds(own * lax.rem(me + d, groups), own)], ts.at[me],
            t_send.at[d - 1], t_recv.at[d - 1], device_id=member_at(d), device_id_type=MESH,
        )

    def send_x(d, c):
        return pltpu.make_async_remote_copy(
            x_ref.at[:, pl.ds(own * lax.rem(me + d, groups) + deep * c, deep)],
            xs.at[groups - d, :, pl.ds(deep * c, deep)],
            x_send.at[d - 1, c], x_recv.at[d - 1, c], device_id=member_at(d), device_id_type=MESH,
        )

    def send_y(d, c):
        return pltpu.make_async_remote_copy(
            ys.at[d, :, pl.ds(deep * c, deep)],
            y_ref.at[:, pl.ds(own * me + deep * c, deep)],
            y_send.at[d - 1, c], y_recv.at[d - 1, c], device_id=member_at(d), device_id_type=MESH,
        )

    order = (1, 3, 2)
    keep_t = pltpu.make_async_copy(t_ref.at[pl.ds(own * me, own)], ts.at[me], t_sem)
    keep_x = pltpu.make_async_copy(x_ref.at[:, pl.ds(own * me, own)], xs.at[0], x_sem)
    for d in order:
        send_t(d).start()
    for c in range(chunks):
        for d in order:
            send_x(d, c).start()
        if c == 0:
            keep_t.start()
            keep_x.start()

    lat = 0.5 * math.pi - (math.pi / (bands * rows)) * (
        (lax.broadcasted_iota(jnp.int32, (rows, cells), 0) + band * rows).astype(jnp.float32) + 0.5
    )
    area[...] = jnp.cos(lat) * (1.0 / mean_cosine(bands * rows))
    part[...] = jnp.zeros_like(part)
    lanes = lax.broadcasted_iota(jnp.int32, (8, 128), 1)

    keep_t.wait()
    keep_x.wait()
    for d in order:
        send_t(d).wait_recv()

    def widen(v, carry):
        tf[v] = jnp.concatenate([ts[p, v].astype(jnp.float32) for p in range(groups)], axis=-1)
        return carry

    lax.fori_loop(0, own, widen, 0)

    def level(v, carry):
        weight = w_ref[own * me + v]
        loss = None
        for start, size in HALVES:
            cut = pl.ds(start, size)
            truth32 = tf[v, :, cut]
            area_here = area[:, cut]

            def member_value(j):
                return xs[j // members, j % members, v, :, cut]

            def put(j, value):
                ys[j // members, j % members, v, :, cut] = value

            block = rank_points(
                [member_value(j) for j in range(groups * members)],
                truth32.astype(jnp.bfloat16), truth32, weight * area_here, member_value, put,
            )
            block = jnp.sum(block * area_here)
            loss = block if loss is None else loss + block
        loss = loss * weight * (1.0 / (bands * rows * cells))
        part[...] += jnp.where(lanes == own * me + v, loss, 0.0)
        return carry

    def chunk(c, carry):
        @pl.when(head & (c == 2))
        def _():
            pl.semaphore_wait(barrier, len(heads))
            for m in range(groups):
                for other in range(CORES):
                    if m + other:
                        greet(opened, {"member": m, "band": band + other})

        for d in order:
            send_x(d, c).wait_recv()
        lax.fori_loop(c * deep, (c + 1) * deep, level, 0)
        for d in order:
            send_y(d, c).start()
        return carry

    lax.fori_loop(0, chunks, chunk, 0)
    keep_y = pltpu.make_async_copy(ys.at[0], y_ref.at[:, pl.ds(own * me, own)], y_sem)
    keep_y.start()

    def move(src, dst, i, peer):
        return pltpu.make_async_remote_copy(
            src, dst, l_send.at[i], l_recv.at[i], device_id=peer, device_id_type=MESH
        )

    def add_up(slots, count):
        total = slots[0]
        for i in range(1, count):
            total = total + slots[i]
        return total

    def exchange(slots, count, mine, at, base):
        slots[mine] = part[...]
        for d in range(1, count):
            move(part, slots.at[mine], base + d - 1, at(d)).start()
        for d in range(1, count):
            move(part, slots.at[mine], base + d - 1, at(d)).wait()
        part[...] = add_up(slots, count)

    @pl.when(jnp.logical_not(head))
    def _():
        pl.semaphore_wait(opened, 1)

    exchange(near, wide * CORES, x * CORES + core, around, 0)
    exchange(far, tall, z, along, wide * CORES)
    exchange(ring, groups, me, member_at, wide * CORES + tall)
    loss_ref[...] = part[0, :levels]

    for d in order:
        send_t(d).wait_send()

    def drain(c, carry):
        for d in order:
            send_x(d, c).wait_send()
            send_y(d, c).wait()
        return carry

    lax.fori_loop(0, chunks, drain, 0)
    keep_y.wait()


def solution(mesh):
    groups, bands = mesh.shape["member"], mesh.shape["band"]
    chunks = 5

    def on_device(predicted_states, observed_truth, height_penalty_factor):
        members, levels, rows, cells = predicted_states.shape
        own = levels // groups
        sizes = (members, levels, rows, cells, groups, bands, chunks)
        wide, tall = bands // (CORES * Z), Z
        dma = pltpu.SemaphoreType.DMA
        peers = wide * CORES + tall + groups
        return pl.pallas_call(
            functools.partial(kernel, sizes),
            out_shape=(
                pltpu.VMEM(predicted_states.shape, jnp.bfloat16),
                jax.ShapeDtypeStruct((levels,), jnp.float32),
            ),
            in_specs=[pl.BlockSpec(memory_space=pltpu.HBM)] * 2 + [pl.BlockSpec(memory_space=pltpu.SMEM)],
            out_specs=(pl.BlockSpec(memory_space=pl.ANY), pl.BlockSpec(memory_space=pltpu.VMEM)),
            scratch_shapes=[
                pltpu.VMEM((groups, members, own, rows, cells), jnp.bfloat16),
                pltpu.VMEM((groups, own, rows, cells // groups), jnp.bfloat16),
                pltpu.VMEM((own, rows, cells), jnp.float32),
                pltpu.VMEM((groups, members, own, rows, cells), jnp.bfloat16),
                pltpu.VMEM((rows, cells), jnp.float32),
                pltpu.VMEM((8, 128), jnp.float32),
                pltpu.VMEM((groups, 8, 128), jnp.float32),
                pltpu.VMEM((wide * CORES, 8, 128), jnp.float32),
                pltpu.VMEM((tall, 8, 128), jnp.float32),
                pltpu.SemaphoreType.REGULAR, pltpu.SemaphoreType.REGULAR,
                dma((groups - 1, chunks)), dma((groups - 1, chunks)), dma,
                dma((groups - 1,)), dma((groups - 1,)), dma,
                dma((groups - 1, chunks)), dma((groups - 1, chunks)), dma,
                dma((peers,)), dma((peers,)),
            ],
            compiler_params=pltpu.CompilerParams(
                collective_id=0, has_side_effects=True, vmem_limit_bytes=56 * 2**20
            ),
        )(predicted_states, observed_truth, height_penalty_factor)

    in_specs = (P("member", None, "band", None), P(None, "band", "member"), P())
    out_specs = (P("member", None, "band", None), P())
    return jax.shard_map(on_device, mesh=mesh, in_specs=in_specs, out_specs=out_specs, check_vma=False)
```

```python
import functools
import math

import jax
import jax.numpy as jnp
import numpy as np
from jax import lax
from jax.experimental import pallas as pl
from jax.experimental.pallas import tpu as pltpu
from jax.sharding import PartitionSpec as P

MESH = pl.DeviceIdType.MESH
ALPHA_FAIR = 0.95
UP = 2.0**120
STEP = 2.0**-13
LANES = 128
FRONT = 1024
PIECES = 1
Z, CORES = 8, 2


def mean_cosine(rows):
    positions = np.arange(rows, dtype=np.float64)
    return float(np.mean(np.cos(0.5 * math.pi - math.pi * (positions + 0.5) / rows)))


def rank_points(members, truth, truth32, weighted, member_value, put):
    count = len(members)
    fair = 1.0 - (1.0 - ALPHA_FAIR) / count
    low, high = jnp.bfloat16(-STEP), jnp.bfloat16(STEP)
    up = [m * jnp.bfloat16(UP) for m in members]
    truth_up = truth * jnp.bfloat16(UP)
    signs = [None] * count
    for j in range(count):
        for k in range(j + 1, count):
            s = jnp.minimum(jnp.maximum(up[j] - up[k], low), high)
            signs[j] = s if signs[j] is None else signs[j] + s
            signs[k] = -s if signs[k] is None else signs[k] - s
    total = None
    for j in range(count):
        beside = jnp.minimum(jnp.maximum(up[j] - truth_up, low), high).astype(jnp.float32)
        grad = beside * (1.0 / STEP / count) - signs[j].astype(jnp.float32) * (
            fair / STEP / (count * (count - 1))
        )
        term = (member_value(j).astype(jnp.float32) - truth32) * grad
        total = term if total is None else total + term
        put(j, (weighted * grad).astype(jnp.bfloat16))
    return total


def kernel(
    sizes, x_ref, t_ref, w_hbm, y_ref, loss_ref, xs, ts, tf, ys, area, part, ring, near, far, w_ref,
    x_edge, xe_out, xe_in, ye_out, ye_in, y_edge, ready, opened, *sems,
):
    members, levels, rows, cells, groups, bands, chunks, early = sizes
    own, deep = levels // groups, levels // groups // chunks
    (x_send, x_recv, x_sem, t_send, t_recv, t_sem, y_send, y_recv, y_sem, l_send, l_recv) = sems[:11]
    (xe_send, xe_recv, xe_sem, ye_send, ye_recv, ye_sem, w_sem) = sems[11:]
    whole = cells // LANES * LANES
    edge = cells - whole
    body, rim = pl.ds(0, whole), pl.ds(whole, edge)
    everyone = groups * members
    me, band = lax.axis_index("member"), lax.axis_index("band")
    core, z, x = lax.rem(band, CORES), lax.rem(band // CORES, Z), band // (CORES * Z)
    wide, tall = bands // (CORES * Z), Z

    def member_at(d):
        return {"member": lax.rem(me + d, groups)}

    def across(d):
        return {"band": (lax.rem(x + d, wide) * Z + z) * CORES + core}

    def around(d):
        i = lax.rem(x * CORES + core + d, wide * CORES)
        return {"band": ((i // CORES) * Z + z) * CORES + lax.rem(i, CORES)}

    def along(d):
        return {"band": (x * Z + lax.rem(z + d, tall)) * CORES + core}

    partner = {"band": band + 1 - 2 * core}
    head = (me == 0) & (core == 0)
    heads = [across(d) for d in range(1, wide)] + [along(d) for d in range(1, tall)]

    keep_w = pltpu.make_async_copy(w_hbm, w_ref, w_sem)
    keep_w.start()
    keep_xe = pltpu.make_async_copy(x_ref.at[:, :, :, rim], x_edge, xe_sem)
    keep_xe.start()
    barrier = pltpu.get_barrier_semaphore()

    def greet(sem, peer):
        pl.semaphore_signal(sem, inc=1, device_id=peer, device_id_type=MESH)

    for d in range(1, groups):

        @pl.when(jnp.logical_not((lax.rem(me + d, groups) == 0) & (core == 0)))
        def _():
            greet(barrier, member_at(d))

    @pl.when(jnp.logical_not((me == 0) & (core == 1)))
    def _():
        greet(barrier, partner)

    @pl.when(jnp.logical_not(head))
    def _():
        pl.semaphore_wait(barrier, groups)

        @pl.when(core == 0)
        def _():
            greet(ready, {"member": 0})

        @pl.when(me == 0)
        def _():
            greet(ready, partner)

    @pl.when(head)
    def _():
        pl.semaphore_wait(ready, groups)
        for peer in heads:
            greet(barrier, peer)

    def send_t(d):
        return pltpu.make_async_remote_copy(
            t_ref.at[pl.ds(own * lax.rem(me + d, groups), own)], ts.at[me],
            t_send.at[d - 1], t_recv.at[d - 1], device_id=member_at(d), device_id_type=MESH,
        )

    def send_x(d, c):
        return pltpu.make_async_remote_copy(
            x_ref.at[:, pl.ds(own * lax.rem(me + d, groups) + deep * c, deep), :, body],
            xs.at[groups - d, :, pl.ds(deep * c, deep)],
            x_send.at[d - 1, c], x_recv.at[d - 1, c], device_id=member_at(d), device_id_type=MESH,
        )

    def send_y(d, c):
        return pltpu.make_async_remote_copy(
            ys.at[d, :, pl.ds(deep * c, deep)],
            y_ref.at[:, pl.ds(own * me + deep * c, deep), :, body],
            y_send.at[d - 1, c], y_recv.at[d - 1, c], device_id=member_at(d), device_id_type=MESH,
        )

    def send_xe(d):
        return pltpu.make_async_remote_copy(
            xe_out.at[d], xe_in.at[groups - d], xe_send.at[d - 1], xe_recv.at[d - 1],
            device_id=member_at(d), device_id_type=MESH,
        )

    def send_ye(d):
        return pltpu.make_async_remote_copy(
            ye_out.at[d], ye_in.at[groups - d], ye_send.at[d - 1], ye_recv.at[d - 1],
            device_id=member_at(d), device_id_type=MESH,
        )

    order = (1, 3, 2)
    keep_t = pltpu.make_async_copy(t_ref.at[pl.ds(own * me, own)], ts.at[me], t_sem)
    keep_x = pltpu.make_async_copy(x_ref.at[:, pl.ds(own * me, own), :, body], xs.at[0], x_sem)
    for d in order:
        send_t(d).start()
    for c in range(early):
        for d in order:
            send_x(d, c).start()
    keep_t.start()
    keep_x.start()

    keep_xe.wait()

    def pack(i, carry):
        d, m = i // members, lax.rem(i, members)
        first = own * lax.rem(me + d, groups)
        row = [x_edge[m, first + v].astype(jnp.float32) for v in range(own)]
        row = jnp.concatenate(row, axis=-1).astype(jnp.bfloat16)

        @pl.when(d == 0)
        def _():
            xe_in[0, m] = row

        @pl.when(d > 0)
        def _():
            xe_out[d, m] = row

        return carry

    lax.fori_loop(0, everyone, pack, 0)
    for d in order:
        send_xe(d).start()
    for c in range(early, chunks):
        for d in order:
            send_x(d, c).start()

    lat = 0.5 * math.pi - (math.pi / (bands * rows)) * (
        (lax.broadcasted_iota(jnp.int32, (rows, cells), 0) + band * rows).astype(jnp.float32) + 0.5
    )
    area[...] = jnp.cos(lat) * (1.0 / mean_cosine(bands * rows))
    part[...] = jnp.zeros_like(part)
    lanes = lax.broadcasted_iota(jnp.int32, (8, 128), 1)

    keep_w.wait()
    keep_t.wait()
    keep_x.wait()
    for d in order:
        send_t(d).wait_recv()

    def widen(v, carry):
        tf[v] = jnp.concatenate([ts[p, v].astype(jnp.float32) for p in range(groups)], axis=-1)
        return carry

    lax.fori_loop(0, own, widen, 0)

    def level(v, carry):
        weight = w_ref[own * me + v]
        loss = None
        for start, size in ((0, FRONT), (FRONT, whole - FRONT)):
            cut = pl.ds(start, size)
            truth32 = tf[v, :, cut]
            area_here = area[:, cut]

            def member_value(j):
                return xs[j // members, j % members, v, :, cut]

            def put(j, value):
                ys[j // members, j % members, v, :, cut] = value

            block = rank_points(
                [member_value(j) for j in range(everyone)],
                truth32.astype(jnp.bfloat16), truth32, weight * area_here, member_value, put,
            )
            block = jnp.sum(block * area_here)
            loss = block if loss is None else loss + block
        loss = loss * weight * (1.0 / (bands * rows * cells))
        part[...] += jnp.where(lanes == own * me + v, loss, 0.0)
        return carry

    def edges():
        for d in order:
            send_xe(d).wait_recv()
        truth32 = jnp.concatenate([tf[v, :, rim] for v in range(own)], axis=-1)
        weights = [w_ref[own * me + v] for v in range(own)]
        area_here = area[:, : own * edge]
        wide_weight = jnp.concatenate([jnp.full((rows, edge), w, jnp.float32) for w in weights], axis=-1)

        def member_value(j):
            return xe_in[j // members, j % members]

        def put(j, value):
            if j < members:
                ye_in[0, j] = value
            else:
                ye_out[j // members, j % members] = value

        block = rank_points(
            [member_value(j) for j in range(everyone)],
            truth32.astype(jnp.bfloat16), truth32, wide_weight * area_here, member_value, put,
        )
        block = block * area_here * wide_weight * (1.0 / (bands * rows * cells))
        loss = part[...]
        for v in range(own):
            loss = loss + jnp.where(lanes == own * me + v, jnp.sum(block[:, edge * v : edge * (v + 1)]), 0.0)
        part[...] = loss
        for d in order:
            send_ye(d).start()

    def chunk(c, carry):
        @pl.when(head & (c == 2))
        def _():
            pl.semaphore_wait(barrier, len(heads))
            for m in range(groups):
                for other in range(CORES):
                    if m + other:
                        greet(opened, {"member": m, "band": band + other})

        for d in order:
            send_x(d, c).wait_recv()
        lax.fori_loop(c * deep, (c + 1) * deep, level, 0)
        for d in order:
            send_y(d, c).start()
        pl.when(c == early - 1)(edges)
        return carry

    lax.fori_loop(0, chunks, chunk, 0)
    keep_y = pltpu.make_async_copy(ys.at[0], y_ref.at[:, pl.ds(own * me, own), :, body], y_sem)
    keep_y.start()

    def move(src, dst, i, peer):
        return pltpu.make_async_remote_copy(
            src, dst, l_send.at[i], l_recv.at[i], device_id=peer, device_id_type=MESH
        )

    def add_up(slots, count):
        total = slots[0]
        for i in range(1, count):
            total = total + slots[i]
        return total

    def hand_out(slots, count, mine, at, base):
        slots[mine] = part[...]
        for d in range(1, count):
            move(part, slots.at[mine], base + d - 1, at(d)).start()

    def take_in(slots, count, mine, at, base):
        for d in range(1, count):
            move(part, slots.at[mine], base + d - 1, at(d)).wait()
        part[...] = add_up(slots, count)

    @pl.when(jnp.logical_not(head))
    def _():
        pl.semaphore_wait(opened, 1)

    by_x = (near, wide * CORES, x * CORES + core, around, 0)
    by_z = (far, tall, z, along, wide * CORES)
    by_y = (ring, groups, me, member_at, wide * CORES + tall)
    hand_out(*by_x)
    take_in(*by_x)
    hand_out(*by_z)
    take_in(*by_z)
    hand_out(*by_y)

    def unpack(i, carry):
        d, m = i // members, lax.rem(i, members)
        first = own * lax.rem(me + d, groups)
        row = ye_in[d, m].astype(jnp.float32)
        for v in range(own):
            y_edge[m, first + v] = row[:, edge * v : edge * (v + 1)].astype(jnp.bfloat16)
        return carry

    for d in order:
        send_ye(d).wait_recv()
    lax.fori_loop(0, everyone, unpack, 0)
    keep_ye = pltpu.make_async_copy(y_edge, y_ref.at[:, :, :, rim], ye_sem)
    keep_ye.start()
    take_in(*by_y)
    loss_ref[...] = part[0, :levels]

    for d in order:
        send_t(d).wait_send()
        send_xe(d).wait_send()
        send_ye(d).wait_send()

    def drain(c, carry):
        for d in order:
            send_x(d, c).wait_send()
            send_y(d, c).wait()
        return carry

    lax.fori_loop(0, chunks, drain, 0)
    keep_y.wait()
    keep_ye.wait()


def settle(pieces, grad_ref, loss_ref, grad_out, loss_out, sems, loss_sem):
    members, levels = grad_ref.shape[:2]
    step = levels // pieces
    copies = [pltpu.make_async_copy(loss_ref, loss_out, loss_sem)]
    for m in range(members):
        for i in range(pieces):
            cut = pl.ds(i * step, step)
            copies.append(pltpu.make_async_copy(grad_ref.at[m, cut], grad_out.at[m, cut], sems.at[m, i]))
    for copy in copies:
        copy.start()
    for copy in copies:
        copy.wait()


def solution(mesh):
    groups, bands = mesh.shape["member"], mesh.shape["band"]
    chunks, early = 5, 2

    def on_device(predicted_states, observed_truth, height_penalty_factor):
        members, levels, rows, cells = predicted_states.shape
        own = levels // groups
        sizes = (members, levels, rows, cells, groups, bands, chunks, early)
        whole = cells // LANES * LANES
        packed = (groups, members, rows, own * (cells - whole))
        wide, tall = bands // (CORES * Z), Z
        dma = pltpu.SemaphoreType.DMA
        peers = wide * CORES + tall + groups
        grad, loss = pl.pallas_call(
            functools.partial(kernel, sizes),
            out_shape=(
                pltpu.VMEM(predicted_states.shape, jnp.bfloat16),
                pltpu.VMEM((levels,), jnp.float32),
            ),
            in_specs=[pl.BlockSpec(memory_space=pltpu.HBM)] * 2 + [pl.BlockSpec(memory_space=pltpu.HBM)],
            out_specs=(pl.BlockSpec(memory_space=pl.ANY), pl.BlockSpec(memory_space=pltpu.VMEM)),
            scratch_shapes=[
                pltpu.VMEM((groups, members, own, rows, whole), jnp.bfloat16),
                pltpu.VMEM((groups, own, rows, cells // groups), jnp.bfloat16),
                pltpu.VMEM((own, rows, cells), jnp.float32),
                pltpu.VMEM((groups, members, own, rows, whole), jnp.bfloat16),
                pltpu.VMEM((rows, cells), jnp.float32),
                pltpu.VMEM((8, 128), jnp.float32),
                pltpu.VMEM((groups, 8, 128), jnp.float32),
                pltpu.VMEM((wide * CORES, 8, 128), jnp.float32),
                pltpu.VMEM((tall, 8, 128), jnp.float32),
                pltpu.SMEM((levels,), jnp.float32),
                pltpu.VMEM((members, levels, rows, cells - whole), jnp.bfloat16),
                pltpu.VMEM(packed, jnp.bfloat16), pltpu.VMEM(packed, jnp.bfloat16),
                pltpu.VMEM(packed, jnp.bfloat16), pltpu.VMEM(packed, jnp.bfloat16),
                pltpu.VMEM((members, levels, rows, cells - whole), jnp.bfloat16),
                pltpu.SemaphoreType.REGULAR, pltpu.SemaphoreType.REGULAR,
                dma((groups - 1, chunks)), dma((groups - 1, chunks)), dma,
                dma((groups - 1,)), dma((groups - 1,)), dma,
                dma((groups - 1, chunks)), dma((groups - 1, chunks)), dma,
                dma((peers,)), dma((peers,)),
                dma((groups - 1,)), dma((groups - 1,)), dma,
                dma((groups - 1,)), dma((groups - 1,)), dma, dma,
            ],
            compiler_params=pltpu.CompilerParams(
                collective_id=0, has_side_effects=True, vmem_limit_bytes=56 * 2**20
            ),
        )(predicted_states, observed_truth, height_penalty_factor)


        return pl.pallas_call(
            functools.partial(settle, PIECES),
            out_shape=(
                jax.ShapeDtypeStruct(grad.shape, grad.dtype),
                jax.ShapeDtypeStruct(loss.shape, loss.dtype),
            ),
            in_specs=[pl.BlockSpec(memory_space=pl.ANY)] * 2,
            out_specs=(pl.BlockSpec(memory_space=pl.ANY),) * 2,
            scratch_shapes=[dma((members, PIECES)), dma],
        )(pltpu.with_memory_space_constraint(grad, pltpu.VMEM), pltpu.with_memory_space_constraint(loss, pltpu.VMEM))

    in_specs = (P("member", None, "band", None), P(None, "band", "member"), P())
    out_specs = (P("member", None, "band", None), P())
    return jax.shard_map(on_device, mesh=mesh, in_specs=in_specs, out_specs=out_specs, check_vma=False)
```

```python
import functools
import math

import jax
import jax.numpy as jnp
import numpy as np
from jax import lax
from jax.experimental import pallas as pl
from jax.experimental.pallas import tpu as pltpu
from jax.sharding import PartitionSpec as P

MESH = pl.DeviceIdType.MESH
ALPHA_FAIR = 0.95
UP = 2.0**120
STEP = 2.0**-13
LANES = 128
INNER = 2 * LANES
PIECES = 1
Z, CORES = 8, 2


def mean_cosine(rows):
    positions = np.arange(rows, dtype=np.float64)
    return float(np.mean(np.cos(0.5 * math.pi - math.pi * (positions + 0.5) / rows)))


def rank_points(members, truth, truth32, weighted, member_value, put):
    count = len(members)
    fair = 1.0 - (1.0 - ALPHA_FAIR) / count
    low, high = jnp.bfloat16(-STEP), jnp.bfloat16(STEP)
    up = [m * jnp.bfloat16(UP) for m in members]
    truth_up = truth * jnp.bfloat16(UP)
    signs = [None] * count
    for j in range(count):
        for k in range(j + 1, count):
            s = jnp.minimum(jnp.maximum(up[j] - up[k], low), high)
            signs[j] = s if signs[j] is None else signs[j] + s
            signs[k] = -s if signs[k] is None else signs[k] - s
    total = None
    for j in range(count):
        beside = jnp.minimum(jnp.maximum(up[j] - truth_up, low), high).astype(jnp.float32)
        grad = beside * (1.0 / STEP / count) - signs[j].astype(jnp.float32) * (
            fair / STEP / (count * (count - 1))
        )
        term = (member_value(j).astype(jnp.float32) - truth32) * grad
        total = term if total is None else total + term
        put(j, (weighted * grad).astype(jnp.bfloat16))
    return total


def kernel(
    sizes, x_ref, t_ref, w_hbm, y_ref, loss_ref, xi, xo, ts, ti, tp, tq, to, yi, yo, area, part, ring, near, far, w_ref,
    x_edge, xe_out, xe_in, ye_out, ye_in, y_edge, ready, opened, *sems,
):
    members, levels, rows, cells, groups, bands, chunks = sizes
    own, deep = levels // groups, levels // chunks
    (x_send, x_recv, x_sem, t_send, t_recv, t_sem, y_send, y_recv, y_sem, l_send, l_recv) = sems[:11]
    (xe_send, xe_recv, xe_sem, ye_send, ye_recv, ye_sem, w_sem) = sems[11:18]
    (xo_send, xo_recv, xo_sem, yo_send, yo_recv, yo_sem, tq_sem) = sems[18:]
    whole = cells // LANES * LANES
    edge = cells - whole
    rim = pl.ds(whole, edge)
    quarter, span = cells // groups, INNER + LANES
    outers = whole // span
    everyone = groups * members
    me, band = lax.axis_index("member"), lax.axis_index("band")
    core, z, x = lax.rem(band, CORES), lax.rem(band // CORES, Z), band // (CORES * Z)
    wide, tall = bands // (CORES * Z), Z

    def member_at(d):
        return {"member": lax.rem(me + d, groups)}

    def across(d):
        return {"band": (lax.rem(x + d, wide) * Z + z) * CORES + core}

    def around(d):
        i = lax.rem(x * CORES + core + d, wide * CORES)
        return {"band": ((i // CORES) * Z + z) * CORES + lax.rem(i, CORES)}

    def along(d):
        return {"band": (x * Z + lax.rem(z + d, tall)) * CORES + core}

    partner = {"band": band + 1 - 2 * core}
    head = (me == 0) & (core == 0)
    heads = [across(d) for d in range(1, wide)] + [along(d) for d in range(1, tall)]

    keep_w = pltpu.make_async_copy(w_hbm, w_ref, w_sem)
    keep_w.start()
    keep_xe = pltpu.make_async_copy(x_ref.at[:, :, :, rim], x_edge, xe_sem)
    keep_xe.start()
    keep_t = pltpu.make_async_copy(t_ref, ts, t_sem)
    keep_t.start()
    barrier = pltpu.get_barrier_semaphore()

    def greet(sem, peer):
        pl.semaphore_signal(sem, inc=1, device_id=peer, device_id_type=MESH)

    for d in range(1, groups):

        @pl.when(jnp.logical_not((lax.rem(me + d, groups) == 0) & (core == 0)))
        def _():
            greet(barrier, member_at(d))

    @pl.when(jnp.logical_not((me == 0) & (core == 1)))
    def _():
        greet(barrier, partner)

    @pl.when(jnp.logical_not(head))
    def _():
        pl.semaphore_wait(barrier, groups)

        @pl.when(core == 0)
        def _():
            greet(ready, {"member": 0})

        @pl.when(me == 0)
        def _():
            greet(ready, partner)

    @pl.when(head)
    def _():
        pl.semaphore_wait(ready, groups)
        for peer in heads:
            greet(barrier, peer)

    def peer_at(d):
        return lax.rem(me + d, groups)

    def deeps(c):
        return pl.ds(deep * c, deep)

    def paired(ref, d, c):
        return ref.at[d, :, c // 2, :, :, pl.ds(pl.multiple_of(INNER * lax.rem(c, 2), LANES), INNER)]

    def inside(q):
        return pl.ds(pl.multiple_of(span * q, LANES), INNER)

    def between(i):
        return pl.ds(INNER + span * i, LANES)

    def remote(src, dst, send, recv, d):
        return pltpu.make_async_remote_copy(src, dst, send, recv, device_id=member_at(d), device_id_type=MESH)

    def send_t(d):
        return remote(tp.at[pl.ds(own * peer_at(d), own)], tq.at[me], t_send.at[d - 1], t_recv.at[d - 1], d)

    def send_x(d, c):
        return remote(
            x_ref.at[:, deeps(c), :, inside(peer_at(d))], paired(xi, groups - d, c),
            x_send.at[d - 1, c], x_recv.at[d - 1, c], d,
        )

    def send_xo(d, i):
        return remote(
            x_ref.at[:, pl.ds(own * peer_at(d), own), :, between(i)],
            xo.at[groups - d, :, :, :, pl.ds(LANES * i, LANES)],
            xo_send.at[d - 1, i], xo_recv.at[d - 1, i], d,
        )

    def send_y(d, c):
        return remote(
            paired(yi, d, c), y_ref.at[:, deeps(c), :, inside(me)],
            y_send.at[d - 1, c], y_recv.at[d - 1, c], d,
        )

    def send_yo(d, i):
        return remote(
            yo.at[d, :, :, :, pl.ds(LANES * i, LANES)], y_ref.at[:, pl.ds(own * me, own), :, between(i)],
            yo_send.at[d - 1, i], yo_recv.at[d - 1, i], d,
        )

    def send_xe(d):
        return pltpu.make_async_remote_copy(
            xe_out.at[d], xe_in.at[groups - d], xe_send.at[d - 1], xe_recv.at[d - 1],
            device_id=member_at(d), device_id_type=MESH,
        )

    def send_ye(d):
        return pltpu.make_async_remote_copy(
            ye_out.at[d], ye_in.at[groups - d], ye_send.at[d - 1], ye_recv.at[d - 1],
            device_id=member_at(d), device_id_type=MESH,
        )

    order = (1, 3, 2)
    keep_x = [
        pltpu.make_async_copy(x_ref.at[:, deeps(c), :, inside(me)], paired(xi, 0, c), x_sem.at[c])
        for c in range(chunks)
    ]
    keep_xo = [
        pltpu.make_async_copy(
            x_ref.at[:, pl.ds(own * me, own), :, between(i)],
            xo.at[0, :, :, :, pl.ds(LANES * i, LANES)], xo_sem.at[i],
        )
        for i in range(outers)
    ]
    for c in range(2):
        for d in order:
            send_x(d, c).start()
    for copy in keep_x + keep_xo:
        copy.start()

    keep_t.wait()
    for q in range(groups):

        @pl.when(me == q)
        def _():
            shift = (span - quarter) * q

            def split(i, carry):
                for c in range(chunks):
                    row = ts[deep * c + i].astype(jnp.float32)
                    ti[c // 2, i, :, pl.ds(INNER * (c % 2), INNER)] = row[:, shift : shift + INNER]
                    rest = row[:, shift + INNER :]
                    if shift:
                        rest = jnp.concatenate([row[:, :shift], rest], axis=-1)
                    tp[deep * c + i] = rest.astype(jnp.bfloat16)
                return carry

            lax.fori_loop(0, deep, split, 0)

    for d in order:
        send_t(d).start()
    keep_tq = pltpu.make_async_copy(tp.at[pl.ds(own * me, own)], tq.at[me], tq_sem)
    keep_tq.start()

    keep_xe.wait()

    def pack(i, carry):
        d, m = i // members, lax.rem(i, members)
        first = own * lax.rem(me + d, groups)
        row = [x_edge[m, first + v].astype(jnp.float32) for v in range(own)]
        row = jnp.concatenate(row, axis=-1).astype(jnp.bfloat16)

        @pl.when(d == 0)
        def _():
            xe_in[0, m] = row

        @pl.when(d > 0)
        def _():
            xe_out[d, m] = row

        return carry

    lax.fori_loop(0, everyone, pack, 0)
    for d in order:
        send_xe(d).start()
    for i in range(outers):
        for d in order:
            send_xo(d, i).start()
    for c in range(2, chunks):
        for d in order:
            send_x(d, c).start()

    lat = 0.5 * math.pi - (math.pi / (bands * rows)) * (
        (lax.broadcasted_iota(jnp.int32, (rows, cells), 0) + band * rows).astype(jnp.float32) + 0.5
    )
    area[...] = jnp.cos(lat) * (1.0 / mean_cosine(bands * rows))
    part[...] = jnp.zeros_like(part)
    lanes = lax.broadcasted_iota(jnp.int32, (8, 128), 1)

    keep_w.wait()
    for copy in keep_x + keep_xo:
        copy.wait()
    keep_tq.wait()

    def level(ats, truth32, member_value, put):
        width = truth32.shape[-1]
        each = width // len(ats)
        weights = [w_ref[at] for at in ats]
        weight = weights[0]
        if len(ats) > 1:
            lane = lax.broadcasted_iota(jnp.int32, (rows, width), 1)
            weight = jnp.where(lane < each, weights[0], weights[1])
        area_here = area[:, pl.ds(0, width)]
        block = rank_points(
            [member_value(j) for j in range(everyone)],
            truth32.astype(jnp.bfloat16), truth32, weight * area_here, member_value, put,
        )
        block = block * area_here
        for i, at in enumerate(ats):
            loss = jnp.sum(block[:, each * i : each * (i + 1)]) * weights[i] * (1.0 / (bands * rows * cells))
            part[...] += jnp.where(lanes == at, loss, 0.0)

    def inner_level(pair, i):
        def member_value(j):
            return xi[j // members, j % members, pair, i]

        def put(j, value):
            yi[j // members, j % members, pair, i] = value

        level([2 * deep * pair + i, 2 * deep * pair + deep + i], ti[pair, i], member_value, put)

    def outer_level(v, carry):
        row = [tq[p, v].astype(jnp.float32) for p in range(groups)]
        to[v] = jnp.concatenate(row, axis=-1)

        def member_value(j):
            return xo[j // members, j % members, v]

        def put(j, value):
            yo[j // members, j % members, v] = value

        level([own * me + v], to[v, :, pl.ds(0, LANES * outers)], member_value, put)
        return carry

    def outside():
        for d in order:
            send_t(d).wait_recv()
        for i in range(outers):
            for d in order:
                send_xo(d, i).wait_recv()
        lax.fori_loop(0, own, outer_level, 0)
        for i in range(outers):
            for d in order:
                send_yo(d, i).start()
        edges()

    def edges():
        for d in order:
            send_xe(d).wait_recv()
        truth32 = jnp.concatenate([to[v, :, pl.ds(LANES * outers, edge)] for v in range(own)], axis=-1)
        weights = [w_ref[own * me + v] for v in range(own)]
        area_here = area[:, : own * edge]
        wide_weight = jnp.concatenate([jnp.full((rows, edge), w, jnp.float32) for w in weights], axis=-1)

        def member_value(j):
            return xe_in[j // members, j % members]

        def put(j, value):
            if j < members:
                ye_in[0, j] = value
            else:
                ye_out[j // members, j % members] = value

        block = rank_points(
            [member_value(j) for j in range(everyone)],
            truth32.astype(jnp.bfloat16), truth32, wide_weight * area_here, member_value, put,
        )
        block = block * area_here * wide_weight * (1.0 / (bands * rows * cells))
        loss = part[...]
        for v in range(own):
            loss = loss + jnp.where(lanes == own * me + v, jnp.sum(block[:, edge * v : edge * (v + 1)]), 0.0)
        part[...] = loss
        for d in order:
            send_ye(d).start()

    def move(src, dst, i, peer):
        return pltpu.make_async_remote_copy(
            src, dst, l_send.at[i], l_recv.at[i], device_id=peer, device_id_type=MESH
        )

    def add_up(slots, count):
        total = slots[0]
        for i in range(1, count):
            total = total + slots[i]
        return total

    def hand_out(slots, count, mine, at, base):
        slots[mine] = part[...]
        for d in range(1, count):
            move(part, slots.at[mine], base + d - 1, at(d)).start()

    def take_in(slots, count, mine, at, base):
        for d in range(1, count):
            move(part, slots.at[mine], base + d - 1, at(d)).wait()
        part[...] = add_up(slots, count)

    by_x = (near, wide * CORES, x * CORES + core, around, 0)
    by_z = (far, tall, z, along, wide * CORES)
    by_y = (ring, groups, me, member_at, wide * CORES + tall)
    def chunk_pair(pair, carry):
        @pl.when(head & (pair == 1))
        def _():
            pl.semaphore_wait(barrier, len(heads))
            for m in range(groups):
                for other in range(CORES):
                    if m + other:
                        greet(opened, {"member": m, "band": band + other})

        for half in range(2):
            for d in order:
                send_x(d, 2 * pair + half).wait_recv()

        def step(i, carry):
            inner_level(pair, i)
            return carry

        lax.fori_loop(0, deep, step, 0)
        @pl.when(pair == chunks // 2 - 1)
        def _():
            @pl.when(jnp.logical_not(head))
            def _():
                pl.semaphore_wait(opened, 1)

            hand_out(*by_x)

        for half in range(2):
            for d in order:
                send_y(d, 2 * pair + half).start()
        pl.when(pair == 0)(outside)
        return carry

    lax.fori_loop(0, chunks // 2, chunk_pair, 0)
    keep_y = [
        pltpu.make_async_copy(paired(yi, 0, c), y_ref.at[:, deeps(c), :, inside(me)], y_sem.at[c])
        for c in range(chunks)
    ]
    keep_y += [
        pltpu.make_async_copy(
            yo.at[0, :, :, :, pl.ds(LANES * i, LANES)],
            y_ref.at[:, pl.ds(own * me, own), :, between(i)], yo_sem.at[i],
        )
        for i in range(outers)
    ]
    for copy in keep_y:
        copy.start()

    take_in(*by_x)
    hand_out(*by_z)
    take_in(*by_z)
    hand_out(*by_y)

    def unpack(i, carry):
        d, m = i // members, lax.rem(i, members)
        first = own * lax.rem(me + d, groups)
        row = ye_in[d, m].astype(jnp.float32)
        for v in range(own):
            y_edge[m, first + v] = row[:, edge * v : edge * (v + 1)].astype(jnp.bfloat16)
        return carry

    for d in order:
        send_ye(d).wait_recv()
    lax.fori_loop(0, everyone, unpack, 0)
    keep_ye = pltpu.make_async_copy(y_edge, y_ref.at[:, :, :, rim], ye_sem)
    keep_ye.start()
    for d in order:
        send_t(d).wait_send()
        send_xe(d).wait_send()
        send_ye(d).wait_send()
        for i in range(outers):
            send_xo(d, i).wait_send()
            send_yo(d, i).wait()

    def drain(c, carry):
        for d in order:
            send_x(d, c).wait_send()
            send_y(d, c).wait()
        return carry

    lax.fori_loop(0, chunks, drain, 0)
    for copy in keep_y:
        copy.wait()
    keep_ye.wait()
    take_in(*by_y)
    loss_ref[...] = part[0, :levels]


def settle(pieces, grad_ref, loss_ref, grad_out, loss_out, sems, loss_sem):
    members, levels = grad_ref.shape[:2]
    step = levels // pieces
    copies = [pltpu.make_async_copy(loss_ref, loss_out, loss_sem)]
    for m in range(members):
        for i in range(pieces):
            cut = pl.ds(i * step, step)
            copies.append(pltpu.make_async_copy(grad_ref.at[m, cut], grad_out.at[m, cut], sems.at[m, i]))
    for copy in copies:
        copy.start()
    for copy in copies:
        copy.wait()


def solution(mesh):
    groups, bands = mesh.shape["member"], mesh.shape["band"]
    chunks = 4

    def on_device(predicted_states, observed_truth, height_penalty_factor):
        members, levels, rows, cells = predicted_states.shape
        own = levels // groups
        sizes = (members, levels, rows, cells, groups, bands, chunks)
        whole = cells // LANES * LANES
        quarter, outers = cells // groups, whole // (INNER + LANES)
        deep = levels // chunks
        inner = (groups, members, chunks // 2, deep, rows, 2 * INNER)
        outer = (groups, members, own, rows, outers * LANES)
        packed = (groups, members, rows, own * (cells - whole))
        wide, tall = bands // (CORES * Z), Z
        dma = pltpu.SemaphoreType.DMA
        peers = wide * CORES + tall + groups
        grad, loss = pl.pallas_call(
            functools.partial(kernel, sizes),
            out_shape=(
                pltpu.VMEM(predicted_states.shape, jnp.bfloat16),
                pltpu.VMEM((levels,), jnp.float32),
            ),
            in_specs=[pl.BlockSpec(memory_space=pltpu.HBM)] * 2 + [pl.BlockSpec(memory_space=pltpu.HBM)],
            out_specs=(pl.BlockSpec(memory_space=pl.ANY), pl.BlockSpec(memory_space=pltpu.VMEM)),
            scratch_shapes=[
                pltpu.VMEM(inner, jnp.bfloat16),
                pltpu.VMEM(outer, jnp.bfloat16),
                pltpu.VMEM((levels, rows, quarter), jnp.bfloat16),
                pltpu.VMEM((chunks // 2, deep, rows, 2 * INNER), jnp.float32),
                pltpu.VMEM((levels, rows, quarter - INNER), jnp.bfloat16),
                pltpu.VMEM((groups, own, rows, quarter - INNER), jnp.bfloat16),
                pltpu.VMEM((own, rows, groups * (quarter - INNER)), jnp.float32),
                pltpu.VMEM(inner, jnp.bfloat16),
                pltpu.VMEM(outer, jnp.bfloat16),
                pltpu.VMEM((rows, cells), jnp.float32),
                pltpu.VMEM((8, 128), jnp.float32),
                pltpu.VMEM((groups, 8, 128), jnp.float32),
                pltpu.VMEM((wide * CORES, 8, 128), jnp.float32),
                pltpu.VMEM((tall, 8, 128), jnp.float32),
                pltpu.SMEM((levels,), jnp.float32),
                pltpu.VMEM((members, levels, rows, cells - whole), jnp.bfloat16),
                pltpu.VMEM(packed, jnp.bfloat16), pltpu.VMEM(packed, jnp.bfloat16),
                pltpu.VMEM(packed, jnp.bfloat16), pltpu.VMEM(packed, jnp.bfloat16),
                pltpu.VMEM((members, levels, rows, cells - whole), jnp.bfloat16),
                pltpu.SemaphoreType.REGULAR, pltpu.SemaphoreType.REGULAR,
                dma((groups - 1, chunks)), dma((groups - 1, chunks)), dma((chunks,)),
                dma((groups - 1,)), dma((groups - 1,)), dma,
                dma((groups - 1, chunks)), dma((groups - 1, chunks)), dma((chunks,)),
                dma((peers,)), dma((peers,)),
                dma((groups - 1,)), dma((groups - 1,)), dma,
                dma((groups - 1,)), dma((groups - 1,)), dma, dma,
                dma((groups - 1, outers)), dma((groups - 1, outers)), dma((outers,)),
                dma((groups - 1, outers)), dma((groups - 1, outers)), dma((outers,)), dma,
            ],
            compiler_params=pltpu.CompilerParams(
                collective_id=0, has_side_effects=True, vmem_limit_bytes=56 * 2**20
            ),
        )(predicted_states, observed_truth, height_penalty_factor)


        return pl.pallas_call(
            functools.partial(settle, PIECES),
            out_shape=(
                jax.ShapeDtypeStruct(grad.shape, grad.dtype),
                jax.ShapeDtypeStruct(loss.shape, loss.dtype),
            ),
            in_specs=[pl.BlockSpec(memory_space=pl.ANY)] * 2,
            out_specs=(pl.BlockSpec(memory_space=pl.ANY),) * 2,
            scratch_shapes=[dma((members, PIECES)), dma],
        )(pltpu.with_memory_space_constraint(grad, pltpu.VMEM), pltpu.with_memory_space_constraint(loss, pltpu.VMEM))

    in_specs = (P("member", None, "band", None), P(None, "band", "member"), P())
    out_specs = (P("member", None, "band", None), P())
    return jax.shard_map(on_device, mesh=mesh, in_specs=in_specs, out_specs=out_specs, check_vma=False)
```

```python
import functools
import math

import jax
import jax.numpy as jnp
import numpy as np
from jax import lax
from jax.experimental import pallas as pl
from jax.experimental.pallas import tpu as pltpu
from jax.sharding import PartitionSpec as P

MESH = pl.DeviceIdType.MESH
ALPHA_FAIR = 0.95
UP = 2.0**120
STEP = 2.0**-13
LANES = 128
INNER = 2 * LANES
PIECES = 1
Z, CORES = 8, 2


def mean_cosine(rows):
    positions = np.arange(rows, dtype=np.float64)
    return float(np.mean(np.cos(0.5 * math.pi - math.pi * (positions + 0.5) / rows)))


def rank_points(members, truth, truth32, weighted, member_value, put):
    count = len(members)
    fair = 1.0 - (1.0 - ALPHA_FAIR) / count
    low, high = jnp.bfloat16(-STEP), jnp.bfloat16(STEP)
    up = [m * jnp.bfloat16(UP) for m in members]
    truth_up = truth * jnp.bfloat16(UP)
    signs = [None] * count
    for j in range(count):
        for k in range(j + 1, count):
            s = jnp.minimum(jnp.maximum(up[j] - up[k], low), high)
            signs[j] = s if signs[j] is None else signs[j] + s
            signs[k] = -s if signs[k] is None else signs[k] - s
    total = None
    for j in range(count):
        beside = jnp.minimum(jnp.maximum(up[j] - truth_up, low), high).astype(jnp.float32)
        grad = beside * (1.0 / STEP / count) - signs[j].astype(jnp.float32) * (
            fair / STEP / (count * (count - 1))
        )
        term = (member_value(j).astype(jnp.float32) - truth32) * grad
        total = term if total is None else total + term
        put(j, (weighted * grad).astype(jnp.bfloat16))
    return total


def kernel(
    sizes, x_ref, t_ref, w_hbm, y_ref, loss_ref, xi, xo, ts, ti, tp, tq, to, yi, yo, area, part, ring, near, far, w_ref,
    x_edge, xe_out, xe_in, ye_out, ye_in, y_edge, ready, opened, *sems,
):
    members, levels, rows, cells, groups, bands, chunks = sizes
    own, deep = levels // groups, levels // chunks
    (x_send, x_recv, x_sem, t_send, t_recv, t_sem, y_send, y_recv, y_sem, l_send, l_recv) = sems[:11]
    (xe_send, xe_recv, xe_sem, ye_send, ye_recv, ye_sem, w_sem) = sems[11:18]
    (xo_send, xo_recv, xo_sem, yo_send, yo_recv, yo_sem, tq_sem) = sems[18:]
    whole = cells // LANES * LANES
    edge = cells - whole
    rim = pl.ds(whole, edge)
    quarter, span = cells // groups, INNER + LANES
    outers = whole // span
    everyone = groups * members
    me, band = lax.axis_index("member"), lax.axis_index("band")
    core, z, x = lax.rem(band, CORES), lax.rem(band // CORES, Z), band // (CORES * Z)
    wide, tall = bands // (CORES * Z), Z

    def member_at(d):
        return {"member": lax.rem(me + d, groups)}

    def across(d):
        return {"band": (lax.rem(x + d, wide) * Z + z) * CORES + core}

    def around(d):
        i = lax.rem(x * CORES + core + d, wide * CORES)
        return {"band": ((i // CORES) * Z + z) * CORES + lax.rem(i, CORES)}

    def along(d):
        return {"band": (x * Z + lax.rem(z + d, tall)) * CORES + core}

    partner = {"band": band + 1 - 2 * core}
    head = (me == 0) & (core == 0)
    heads = [across(d) for d in range(1, wide)] + [along(d) for d in range(1, tall)]

    keep_w = pltpu.make_async_copy(w_hbm, w_ref, w_sem)
    keep_w.start()
    keep_xe = pltpu.make_async_copy(x_ref.at[:, :, :, rim], x_edge, xe_sem)
    keep_xe.start()
    keep_t = pltpu.make_async_copy(t_ref, ts, t_sem)
    keep_t.start()
    barrier = pltpu.get_barrier_semaphore()

    def greet(sem, peer):
        pl.semaphore_signal(sem, inc=1, device_id=peer, device_id_type=MESH)

    for d in range(1, groups):

        @pl.when(jnp.logical_not((lax.rem(me + d, groups) == 0) & (core == 0)))
        def _():
            greet(barrier, member_at(d))

    @pl.when(jnp.logical_not((me == 0) & (core == 1)))
    def _():
        greet(barrier, partner)

    @pl.when(jnp.logical_not(head))
    def _():
        pl.semaphore_wait(barrier, groups)

        @pl.when(core == 0)
        def _():
            greet(ready, {"member": 0})

        @pl.when(me == 0)
        def _():
            greet(ready, partner)

    @pl.when(head)
    def _():
        pl.semaphore_wait(ready, groups)
        for peer in heads:
            greet(barrier, peer)

    def peer_at(d):
        return lax.rem(me + d, groups)

    def deeps(c):
        return pl.ds(deep * c, deep)

    def paired(ref, d, c):
        return ref.at[d, :, c // 2, :, :, pl.ds(pl.multiple_of(INNER * lax.rem(c, 2), LANES), INNER)]

    def inside(q):
        return pl.ds(pl.multiple_of(span * q, LANES), INNER)

    def between(i):
        return pl.ds(INNER + span * i, LANES)

    def remote(src, dst, send, recv, d):
        return pltpu.make_async_remote_copy(src, dst, send, recv, device_id=member_at(d), device_id_type=MESH)

    def send_t(d):
        return remote(tp.at[pl.ds(own * peer_at(d), own)], tq.at[me], t_send.at[d - 1], t_recv.at[d - 1], d)

    def send_x(d, c):
        return remote(
            x_ref.at[:, deeps(c), :, inside(peer_at(d))], paired(xi, groups - d, c),
            x_send.at[d - 1, c], x_recv.at[d - 1, c], d,
        )

    def send_xo(d, i):
        return remote(
            x_ref.at[:, pl.ds(own * peer_at(d), own), :, between(i)],
            xo.at[groups - d, :, :, :, pl.ds(LANES * i, LANES)],
            xo_send.at[d - 1, i], xo_recv.at[d - 1, i], d,
        )

    def send_y(d, c):
        return remote(
            paired(yi, d, c), y_ref.at[:, deeps(c), :, inside(me)],
            y_send.at[d - 1, c], y_recv.at[d - 1, c], d,
        )

    def send_yo(d, i):
        return remote(
            yo.at[d, :, :, :, pl.ds(LANES * i, LANES)], y_ref.at[:, pl.ds(own * me, own), :, between(i)],
            yo_send.at[d - 1, i], yo_recv.at[d - 1, i], d,
        )

    def send_xe(d):
        return pltpu.make_async_remote_copy(
            xe_out.at[d], xe_in.at[groups - d], xe_send.at[d - 1], xe_recv.at[d - 1],
            device_id=member_at(d), device_id_type=MESH,
        )

    def send_ye(d):
        return pltpu.make_async_remote_copy(
            ye_out.at[d], ye_in.at[groups - d], ye_send.at[d - 1], ye_recv.at[d - 1],
            device_id=member_at(d), device_id_type=MESH,
        )

    order = (1, 3, 2)
    keep_x = [
        pltpu.make_async_copy(x_ref.at[:, deeps(c), :, inside(me)], paired(xi, 0, c), x_sem.at[c])
        for c in range(chunks)
    ]
    keep_xo = [
        pltpu.make_async_copy(
            x_ref.at[:, pl.ds(own * me, own), :, between(i)],
            xo.at[0, :, :, :, pl.ds(LANES * i, LANES)], xo_sem.at[i],
        )
        for i in range(outers)
    ]
    for c in range(2):
        for d in order:
            send_x(d, c).start()
    for copy in keep_x + keep_xo:
        copy.start()

    keep_t.wait()
    for q in range(groups):

        @pl.when(me == q)
        def _():
            shift = (span - quarter) * q

            def split(i, carry):
                for c in range(chunks):
                    row = ts[deep * c + i].astype(jnp.float32)
                    ti[c // 2, i, :, pl.ds(INNER * (c % 2), INNER)] = row[:, shift : shift + INNER]
                    rest = row[:, shift + INNER :]
                    if shift:
                        rest = jnp.concatenate([row[:, :shift], rest], axis=-1)
                    tp[deep * c + i] = rest.astype(jnp.bfloat16)
                return carry

            lax.fori_loop(0, deep, split, 0)

    for d in order:
        send_t(d).start()
    keep_tq = pltpu.make_async_copy(tp.at[pl.ds(own * me, own)], tq.at[me], tq_sem)
    keep_tq.start()

    keep_xe.wait()

    def pack(i, carry):
        d, m = i // members, lax.rem(i, members)
        first = own * lax.rem(me + d, groups)
        row = [x_edge[m, first + v].astype(jnp.float32) for v in range(own)]
        row = jnp.concatenate(row, axis=-1).astype(jnp.bfloat16)

        @pl.when(d == 0)
        def _():
            xe_in[0, m] = row

        @pl.when(d > 0)
        def _():
            xe_out[d, m] = row

        return carry

    lax.fori_loop(0, everyone, pack, 0)
    for d in order:
        send_xe(d).start()
    for i in range(outers):
        for d in order:
            send_xo(d, i).start()
    for c in range(2, chunks):
        for d in order:
            send_x(d, c).start()

    lat = 0.5 * math.pi - (math.pi / (bands * rows)) * (
        (lax.broadcasted_iota(jnp.int32, (rows, cells), 0) + band * rows).astype(jnp.float32) + 0.5
    )
    area[...] = jnp.cos(lat) * (1.0 / mean_cosine(bands * rows))
    part[...] = jnp.zeros_like(part)
    lanes = lax.broadcasted_iota(jnp.int32, (8, 128), 1)

    keep_w.wait()
    for copy in keep_x + keep_xo:
        copy.wait()
    keep_tq.wait()

    def level(ats, truth32, member_value, put):
        width = truth32.shape[-1]
        each = width // len(ats)
        weights = [w_ref[at] for at in ats]
        weight = weights[0]
        if len(ats) > 1:
            lane = lax.broadcasted_iota(jnp.int32, (rows, width), 1)
            weight = jnp.where(lane < each, weights[0], weights[1])
        area_here = area[:, pl.ds(0, width)]
        block = rank_points(
            [member_value(j) for j in range(everyone)],
            truth32.astype(jnp.bfloat16), truth32, weight * area_here, member_value, put,
        )
        block = block * area_here
        for i, at in enumerate(ats):
            loss = jnp.sum(block[:, each * i : each * (i + 1)]) * weights[i] * (1.0 / (bands * rows * cells))
            part[...] += jnp.where(lanes == at, loss, 0.0)

    def inner_level(pair, i):
        def member_value(j):
            return xi[j // members, j % members, pair, i]

        def put(j, value):
            yi[j // members, j % members, pair, i] = value

        level([2 * deep * pair + i, 2 * deep * pair + deep + i], ti[pair, i], member_value, put)

    def outer_level(v, carry):
        row = [tq[p, v].astype(jnp.float32) for p in range(groups)]
        to[v] = jnp.concatenate(row, axis=-1)

        def member_value(j):
            return xo[j // members, j % members, v]

        def put(j, value):
            yo[j // members, j % members, v] = value

        level([own * me + v], to[v, :, pl.ds(0, LANES * outers)], member_value, put)
        return carry

    def outside():
        for d in order:
            send_t(d).wait_recv()
        for i in range(outers):
            for d in order:
                send_xo(d, i).wait_recv()
        lax.fori_loop(0, own, outer_level, 0)
        for i in range(outers):
            for d in order:
                send_yo(d, i).start()
        edges()

    def edges():
        for d in order:
            send_xe(d).wait_recv()
        truth32 = jnp.concatenate([to[v, :, pl.ds(LANES * outers, edge)] for v in range(own)], axis=-1)
        weights = [w_ref[own * me + v] for v in range(own)]
        area_here = area[:, : own * edge]
        wide_weight = jnp.concatenate([jnp.full((rows, edge), w, jnp.float32) for w in weights], axis=-1)

        def member_value(j):
            return xe_in[j // members, j % members]

        def put(j, value):
            if j < members:
                ye_in[0, j] = value
            else:
                ye_out[j // members, j % members] = value

        block = rank_points(
            [member_value(j) for j in range(everyone)],
            truth32.astype(jnp.bfloat16), truth32, wide_weight * area_here, member_value, put,
        )
        block = block * area_here * wide_weight * (1.0 / (bands * rows * cells))
        loss = part[...]
        for v in range(own):
            loss = loss + jnp.where(lanes == own * me + v, jnp.sum(block[:, edge * v : edge * (v + 1)]), 0.0)
        part[...] = loss
        for d in order:
            send_ye(d).start()

    def move(src, dst, i, peer):
        return pltpu.make_async_remote_copy(
            src, dst, l_send.at[i], l_recv.at[i], device_id=peer, device_id_type=MESH
        )

    def add_up(slots, count):
        total = slots[0]
        for i in range(1, count):
            total = total + slots[i]
        return total

    def hand_out(slots, count, mine, at, base):
        slots[mine] = part[...]
        for d in range(1, count):
            move(part, slots.at[mine], base + d - 1, at(d)).start()

    def take_in(slots, count, mine, at, base):
        for d in range(1, count):
            move(part, slots.at[mine], base + d - 1, at(d)).wait()
        part[...] = add_up(slots, count)

    by_x = (near, wide * CORES, x * CORES + core, around, 0)
    by_z = (far, tall, z, along, wide * CORES)
    by_y = (ring, groups, me, member_at, wide * CORES + tall)
    def chunk_pair(pair, carry):
        @pl.when(head & (pair == 1))
        def _():
            pl.semaphore_wait(barrier, len(heads))
            for m in range(groups):
                for other in range(CORES):
                    if m + other:
                        greet(opened, {"member": m, "band": band + other})

        for half in range(2):
            for d in order:
                send_x(d, 2 * pair + half).wait_recv()

        def step(i, carry):
            inner_level(pair, i)
            return carry

        lax.fori_loop(0, deep, step, 0, unroll=5)
        @pl.when(pair == chunks // 2 - 1)
        def _():
            @pl.when(jnp.logical_not(head))
            def _():
                pl.semaphore_wait(opened, 1)

            hand_out(*by_x)

        for half in range(2):
            for d in order:
                send_y(d, 2 * pair + half).start()
        pl.when(pair == 0)(outside)
        return carry

    lax.fori_loop(0, chunks // 2, chunk_pair, 0)
    keep_y = [
        pltpu.make_async_copy(paired(yi, 0, c), y_ref.at[:, deeps(c), :, inside(me)], y_sem.at[c])
        for c in range(chunks)
    ]
    keep_y += [
        pltpu.make_async_copy(
            yo.at[0, :, :, :, pl.ds(LANES * i, LANES)],
            y_ref.at[:, pl.ds(own * me, own), :, between(i)], yo_sem.at[i],
        )
        for i in range(outers)
    ]
    for copy in keep_y:
        copy.start()

    take_in(*by_x)
    hand_out(*by_z)
    take_in(*by_z)
    hand_out(*by_y)

    def unpack(i, carry):
        d, m = i // members, lax.rem(i, members)
        first = own * lax.rem(me + d, groups)
        row = ye_in[d, m].astype(jnp.float32)
        for v in range(own):
            y_edge[m, first + v] = row[:, edge * v : edge * (v + 1)].astype(jnp.bfloat16)
        return carry

    for d in order:
        send_ye(d).wait_recv()
    lax.fori_loop(0, everyone, unpack, 0)
    keep_ye = pltpu.make_async_copy(y_edge, y_ref.at[:, :, :, rim], ye_sem)
    keep_ye.start()
    for d in order:
        send_t(d).wait_send()
        send_xe(d).wait_send()
        send_ye(d).wait_send()
        for i in range(outers):
            send_xo(d, i).wait_send()
            send_yo(d, i).wait()

    def drain(c, carry):
        for d in order:
            send_x(d, c).wait_send()
            send_y(d, c).wait()
        return carry

    lax.fori_loop(0, chunks, drain, 0)
    for copy in keep_y:
        copy.wait()
    keep_ye.wait()
    take_in(*by_y)
    loss_ref[...] = part[0, :levels]


def settle(pieces, grad_ref, loss_ref, grad_out, loss_out, sems, loss_sem):
    members, levels = grad_ref.shape[:2]
    step = levels // pieces
    copies = [pltpu.make_async_copy(loss_ref, loss_out, loss_sem)]
    for m in range(members):
        for i in range(pieces):
            cut = pl.ds(i * step, step)
            copies.append(pltpu.make_async_copy(grad_ref.at[m, cut], grad_out.at[m, cut], sems.at[m, i]))
    for copy in copies:
        copy.start()
    for copy in copies:
        copy.wait()


def solution(mesh):
    groups, bands = mesh.shape["member"], mesh.shape["band"]
    chunks = 4

    def on_device(predicted_states, observed_truth, height_penalty_factor):
        members, levels, rows, cells = predicted_states.shape
        own = levels // groups
        sizes = (members, levels, rows, cells, groups, bands, chunks)
        whole = cells // LANES * LANES
        quarter, outers = cells // groups, whole // (INNER + LANES)
        deep = levels // chunks
        inner = (groups, members, chunks // 2, deep, rows, 2 * INNER)
        outer = (groups, members, own, rows, outers * LANES)
        packed = (groups, members, rows, own * (cells - whole))
        wide, tall = bands // (CORES * Z), Z
        dma = pltpu.SemaphoreType.DMA
        peers = wide * CORES + tall + groups
        grad, loss = pl.pallas_call(
            functools.partial(kernel, sizes),
            out_shape=(
                pltpu.VMEM(predicted_states.shape, jnp.bfloat16),
                pltpu.VMEM((levels,), jnp.float32),
            ),
            in_specs=[pl.BlockSpec(memory_space=pltpu.HBM)] * 2 + [pl.BlockSpec(memory_space=pltpu.HBM)],
            out_specs=(pl.BlockSpec(memory_space=pl.ANY), pl.BlockSpec(memory_space=pltpu.VMEM)),
            scratch_shapes=[
                pltpu.VMEM(inner, jnp.bfloat16),
                pltpu.VMEM(outer, jnp.bfloat16),
                pltpu.VMEM((levels, rows, quarter), jnp.bfloat16),
                pltpu.VMEM((chunks // 2, deep, rows, 2 * INNER), jnp.float32),
                pltpu.VMEM((levels, rows, quarter - INNER), jnp.bfloat16),
                pltpu.VMEM((groups, own, rows, quarter - INNER), jnp.bfloat16),
                pltpu.VMEM((own, rows, groups * (quarter - INNER)), jnp.float32),
                pltpu.VMEM(inner, jnp.bfloat16),
                pltpu.VMEM(outer, jnp.bfloat16),
                pltpu.VMEM((rows, cells), jnp.float32),
                pltpu.VMEM((8, 128), jnp.float32),
                pltpu.VMEM((groups, 8, 128), jnp.float32),
                pltpu.VMEM((wide * CORES, 8, 128), jnp.float32),
                pltpu.VMEM((tall, 8, 128), jnp.float32),
                pltpu.SMEM((levels,), jnp.float32),
                pltpu.VMEM((members, levels, rows, cells - whole), jnp.bfloat16),
                pltpu.VMEM(packed, jnp.bfloat16), pltpu.VMEM(packed, jnp.bfloat16),
                pltpu.VMEM(packed, jnp.bfloat16), pltpu.VMEM(packed, jnp.bfloat16),
                pltpu.VMEM((members, levels, rows, cells - whole), jnp.bfloat16),
                pltpu.SemaphoreType.REGULAR, pltpu.SemaphoreType.REGULAR,
                dma((groups - 1, chunks)), dma((groups - 1, chunks)), dma((chunks,)),
                dma((groups - 1,)), dma((groups - 1,)), dma,
                dma((groups - 1, chunks)), dma((groups - 1, chunks)), dma((chunks,)),
                dma((peers,)), dma((peers,)),
                dma((groups - 1,)), dma((groups - 1,)), dma,
                dma((groups - 1,)), dma((groups - 1,)), dma, dma,
                dma((groups - 1, outers)), dma((groups - 1, outers)), dma((outers,)),
                dma((groups - 1, outers)), dma((groups - 1, outers)), dma((outers,)), dma,
            ],
            compiler_params=pltpu.CompilerParams(
                collective_id=0, has_side_effects=True, vmem_limit_bytes=56 * 2**20
            ),
        )(predicted_states, observed_truth, height_penalty_factor)


        return pl.pallas_call(
            functools.partial(settle, PIECES),
            out_shape=(
                jax.ShapeDtypeStruct(grad.shape, grad.dtype),
                jax.ShapeDtypeStruct(loss.shape, loss.dtype),
            ),
            in_specs=[pl.BlockSpec(memory_space=pl.ANY)] * 2,
            out_specs=(pl.BlockSpec(memory_space=pl.ANY),) * 2,
            scratch_shapes=[dma((members, PIECES)), dma],
        )(pltpu.with_memory_space_constraint(grad, pltpu.VMEM), pltpu.with_memory_space_constraint(loss, pltpu.VMEM))

    in_specs = (P("member", None, "band", None), P(None, "band", "member"), P())
    out_specs = (P("member", None, "band", None), P())
    return jax.shard_map(on_device, mesh=mesh, in_specs=in_specs, out_specs=out_specs, check_vma=False)
```
